512 devices in a mesh: row: 128 (over z_lo, x, y, core), rep: 4 (over z_hi).
Axes of the slice: x: 4, y: 4, z: 16 (z_hi: 4, z_lo: 4; z = z_hi * 4 + z_lo), core: 2. Of those that a mesh axis runs over, the one named last changes fastest.
Arguments:
- grad_out: bfloat16 [65536, 256], P(('row', 'rep')), may hold values from -6 to 6
- pre_act: bfloat16 [65536, 256], P(('row', 'rep')), may hold values from -8 to 8
- features: bfloat16 [65536, 256], P(('row', 'rep')), may hold values from -6 to 6
- weight: bfloat16 [256, 256], replicated, may hold values from -0.375 to 0.375
- tile_values: bfloat16 [128, 4, 48, 128, 128], P('row', 'rep'), may hold values from -2.5 to 2.5
- tile_rows: int32 [128, 4, 48], P('row', 'rep'), may hold values from 0 to 3
- tile_cols: int32 [128, 4, 48], P('row', 'rep'), may hold values from 0 to 127
- tile_count: int32 [128, 4], P('row', 'rep'), may hold values from 6 to 48, as said below
- degrees: int32 [65536], P(('row', 'rep')), may hold values from 1 to 64
Outputs:
- grad_features: bfloat16 [65536, 256], P(('row', 'rep'))
- grad_weight: float32 [256, 256], replicated
The draws below stay inside these ranges and needn't reach their ends.
Inputs may be any that keep to these rules, and one draw needn't show every extreme that they name: `tile_count`: slot counts of a device; some device uses all 48 slots.
All inputs are finite; a program needn't handle non-finite values.
Results may differ from the reference program's by a relative error of at most 0.015.
Values may be sent and summed in bfloat16 or wider, within the bound.
A program may use at most 64 MiB of HBM per device.

```python
import jax
import jax.numpy as jnp
from jax import lax

F = 256
BLOCK = 128
SLOTS = 48
NODES = 65536
N_ROW = 128
N_REP = 4


def draw_tile_count(key, part):
    key = jax.random.fold_in(key, 11)
    key_base, key_heavy, key_hub, key_full = jax.random.split(key, 4)
    lowest = max(1, SLOTS // 8)
    base_count = jax.random.randint(key_base, (N_ROW, N_REP), lowest, SLOTS // 2 + 1)
    heavy_count = jax.random.randint(key_heavy, (N_ROW, N_REP), 3 * SLOTS // 4, SLOTS + 1)
    hub_pick = jax.random.randint(key_hub, (N_ROW, N_REP), 0, 8) == 0
    counts = jnp.where(hub_pick, heavy_count, base_count).reshape(-1)
    full_device = jax.random.randint(key_full, (), 0, N_ROW * N_REP)
    counts = counts.at[full_device].set(SLOTS)
    return counts.reshape(N_ROW, N_REP).astype(jnp.int32)


def with_ends(result, rng, low, high):
    longest = result.shape.index(max(result.shape))
    spots = []
    for shift in (0, 1):
        where = [jax.random.randint(jax.random.fold_in(rng, axis), (), 0, length) for axis, length in enumerate(result.shape)]
        where[longest] = (where[longest] + shift) % result.shape[longest]
        spots.append(tuple(where))
    return result.at[spots[0]].set(low).at[spots[1]].set(high)


def shard_levels(rng, dims, cuts, least, largest):
    def one(position, blocks):
        steps = jax.random.uniform(jax.random.fold_in(jax.random.fold_in(rng, 6), position), (blocks,), jnp.float32, least / len(cuts), largest / len(cuts))
        return jnp.repeat(jnp.exp(steps), dims[position] // blocks).reshape((-1,) + (1,) * (len(dims) - position - 1))

    factor_of = one(*cuts[0])
    for cut in cuts[1:]:
        factor_of = factor_of * one(*cut)
    return factor_of


def gaussian(rng, dims, scale, limit, cuts=(), held_as=jnp.bfloat16):
    entries = scale * jax.random.normal(rng, dims, jnp.float32)
    if cuts:
        entries = entries * shard_levels(rng, dims, cuts, -0.22, 0.18)
    return jnp.clip(entries, -limit, limit).astype(held_as)


def setup_inputs(seed: int = 0) -> dict:
    key_of = jax.random.split(jax.random.key(seed), 10)
    return {
        "grad_out": gaussian(key_of[0], (NODES, F), 1.0, 6.0, ((0, 512),)),
        "pre_act": gaussian(key_of[1], (NODES, F), 1.5, 8.0, ((0, 512),)),
        "features": gaussian(key_of[2], (NODES, F), 1.0, 6.0, ((0, 512),)),
        "weight": gaussian(key_of[3], (F, F), F ** -0.5, 0.375),
        "tile_values": gaussian(key_of[4], (N_ROW, N_REP, SLOTS, BLOCK, BLOCK), (32.0 / (SLOTS * BLOCK) ** 0.5), 2.5, ((0, 128), (1, 4))),
        "tile_rows": with_ends(jax.random.randint(key_of[5], (N_ROW, N_REP, SLOTS), 0, N_REP), jax.random.fold_in(key_of[5], 1), 0, N_REP - 1).astype(jnp.int32),
        "tile_cols": with_ends(jax.random.randint(key_of[6], (N_ROW, N_REP, SLOTS), 0, N_ROW), jax.random.fold_in(key_of[6], 1), 0, N_ROW - 1).astype(jnp.int32),
        "tile_count": draw_tile_count(jax.random.fold_in(key_of[9], 71), 0),
        "degrees": with_ends(jax.random.randint(key_of[8], (NODES,), 1, 65), jax.random.fold_in(key_of[8], 1), 1, 64).astype(jnp.int32),
    }


def reference(grad_out, pre_act, features, weight, tile_values, tile_rows, tile_cols, tile_count, degrees):
    inv_sqrt = lax.rsqrt(degrees.astype(jnp.float32))
    preact = pre_act.astype(jnp.float32)
    gate_sig = jax.nn.sigmoid(preact)
    grad_pre = grad_out.astype(jnp.float32) * gate_sig * (1.0 + preact * (1.0 - gate_sig))
    scaled_grad = (inv_sqrt[:, None] * grad_pre).astype(jnp.bfloat16)
    grad_blocks = scaled_grad.reshape(N_ROW, N_REP, BLOCK, F)
    slot_ids = jnp.arange(SLOTS).astype(jnp.int32)
    live_slots = slot_ids[None, None, :] < tile_count[:, :, None]
    rep_ids = jnp.arange(N_REP).astype(jnp.int32)
    row_hot = ((tile_rows[..., None] == rep_ids[None, None, None, :]) & live_slots[..., None]).astype(jnp.float32)

    def row_device(row_dev):
        tile_vals = tile_values[row_dev].astype(jnp.float32)
        col_index = tile_cols[row_dev]
        picked = grad_blocks[col_index, rep_ids[:, None]].astype(jnp.float32)
        product = jnp.einsum('ksij,ksjf->ksif', tile_vals, picked)
        return jnp.einsum('ksr,ksif->rif', row_hot[row_dev], product)
    partials = lax.map(row_device, jnp.arange(N_ROW).astype(jnp.int32))
    grad_agg = (inv_sqrt.reshape(N_ROW, N_REP, BLOCK, 1) * partials).reshape(NODES, F).astype(jnp.bfloat16)
    grad_features = lax.dot_general(grad_agg, weight, (((1,), (1,)), ((), ())), preferred_element_type=jnp.float32).astype(jnp.bfloat16)
    grad_weight = lax.dot_general(features, grad_agg, (((0,), (0,)), ((), ())), preferred_element_type=jnp.float32)
    return (grad_features, grad_weight)
```

```python
import jax
import jax.numpy as jnp
from jax import lax
from jax.experimental import pallas as pl
from jax.experimental.pallas import tpu as pltpu
from jax.sharding import PartitionSpec as P

MESH = pl.DeviceIdType.MESH
BF16 = jnp.bfloat16
F32 = jnp.float32
SLOTS = 48
DIRS = (1, -1)
CLASSES = (0, 1)
DIR_AT = {1: 0, -1: 1}
PIECE_AT = {0: 0, -1: 1, 1: 2, 2: 3}
LAYER_ORDER = [[1, 2, 3], [0, 2, 3], [3, 1, 0], [2, 1, 0]]
LAYER_CODE = sum(
    LAYER_ORDER[z][j] * 4 ** (z * 3 + j) for z in range(4) for j in range(3)
)
STEPS = (
    ("begin", 0), ("stage", 0), ("middle", 0), ("begin", 1), ("stage", 1), ("begin", 2), ("middle", 1),
    ("begin", 3), ("stage", 2), ("middle", 2), ("end", 0), ("middle", 3), ("end", 1), ("finish", 0),
    ("end", 2), ("finish", 1), ("end", 3), ("finish", 2), ("finish", 3),
)


def kernel(
    grad_hbm, pre_hbm, feat_hbm, weight_hbm, tiles_hbm, rows_ref, cols_ref, count_ref,
    degrees_ref, gf_out, gw_out,
    G, grad_v, pre_v, feat_v, weight_v, tiles_v, stacked, total, feat_t, part16, part_in,
    w16, w_in1, w_in2, w_in3,
    load_sem, z_send, z_recv, s1_send, s1_recv, s2_send, s2_recv, s3_send, s3_recv,
    s4_send, s4_recv, sib_send, sib_recv, feat_send, feat_recv, part_send, part_recv,
    w1_send, w1_recv, w2_send, w2_recv, w3_send, w3_recv, ring1, ring2, ring3,
):
    row = lax.axis_index("row")
    rep = lax.axis_index("rep")
    c = row % 2
    y = (row // 2) % 4
    x = (row // 8) % 4
    zl = row // 32
    layer_at = row % 32

    def dev(at_z, at_x, at_y, at_c):
        return (((at_z * 4 + at_x) * 4 + at_y) * 2 + at_c, rep)

    xs = {0: x, 1: (x + 1) % 4, 2: (x + 2) % 4, -1: (x + 3) % 4}
    ys = {0: y, 1: (y + 1) % 4, 2: (y + 2) % 4, -1: (y + 3) % 4}
    near = {
        (0, 1): dev(zl, xs[1], y, c),
        (0, -1): dev(zl, xs[-1], y, c),
        (1, 1): dev(zl, x, ys[1], c),
        (1, -1): dev(zl, x, ys[-1], c),
    }
    sibling = dev(zl, x, y, 1 - c)
    z_mates = [dev((zl + j) % 4, x, y, c) for j in (1, 2, 3)]
    rep_mates = [(row, (rep + j) % 4) for j in (1, 2, 3)]
    far = {0: dev(zl, xs[2], y, c), 1: dev(zl, x, ys[2], c)}
    z_at = rep * 4 + zl

    def ring(step):
        at = (z_at + step + 16) % 16
        return ((at % 4) * 32 + layer_at, at // 4)

    def signal(sem, to):
        pl.semaphore_signal(sem, inc=1, device_id=to, device_id_type=MESH)


    loads = [
        pltpu.make_async_copy(src, dst, load_sem.at[i])
        for i, (src, dst) in enumerate(
            [
                (grad_hbm, grad_v),
                (pre_hbm, pre_v),
                (feat_hbm, feat_v),
                (tiles_hbm, tiles_v),
                (weight_hbm, weight_v),
            ]
        )
    ]
    for load in loads:
        load.start()

    barrier = pltpu.get_barrier_semaphore()
    peers = list(near.values()) + list(far.values()) + [sibling] + z_mates + [ring(1), ring(-1)]
    for peer in peers:
        signal(barrier, peer)

    inv_row = lax.rsqrt(degrees_ref[...].astype(F32))
    inv_half = jnp.broadcast_to(inv_row, (128, 128)).T
    inv = jnp.concatenate([inv_half, inv_half], axis=1)

    loads[0].wait()
    loads[1].wait()
    pre = pre_v[...].astype(F32)
    gate = jax.nn.sigmoid(pre)
    grad_pre = grad_v[...].astype(F32) * gate * (1.0 + pre * (1.0 - gate))
    G[c, zl, x, y] = (inv * grad_pre).astype(BF16)

    pl.semaphore_wait(barrier, len(peers))
    signal(ring1, ring(1))
    signal(ring1, ring(-1))

    sends = []

    def copy(src, dst, send_sem, recv_sem, to):
        return pltpu.make_async_remote_copy(
            src_ref=src,
            dst_ref=dst,
            send_sem=send_sem,
            recv_sem=recv_sem,
            device_id=to,
            device_id_type=MESH,
        )

    def same(ref, send_sem, recv_sem, to):
        return copy(ref, ref, send_sem, recv_sem, to)

    def go(cp):
        cp.start()
        sends.append(cp)

    layers = [zl] + [(LAYER_CODE // 4 ** j // _power(zl)) % 4 for j in range(3)]

    def piece(k, layer, dp, dq, low, size):
        dx, dy = (dp, dq) if k == 0 else (dq, dp)
        return G.at[c, layer, xs[dx], ys[dy], pl.ds(k * 64 + low, size)]

    def first(j, k, d, dp):
        at = (j, k, DIR_AT[d])
        return same(piece(k, layers[j], dp, 0, 0, 64), s1_send.at[at], s1_recv.at[at], near[k, d])

    def first_far(j, k, dp):
        at = (j, k)
        return same(piece(k, layers[j], dp, 0, 0, 64), s2_send.at[at], s2_recv.at[at], far[k])

    def second(j, k, dp, d, dq):
        at = (j, k, PIECE_AT[dp], DIR_AT[d])
        return same(
            piece(k, layers[j], dp, dq, 0, 64), s3_send.at[at], s3_recv.at[at], near[1 - k, d]
        )

    def second_far(j, k, dp, d, dq):
        at = (j, k, PIECE_AT[dp], DIR_AT[d])
        low = 0 if d == 1 else 32
        return same(
            piece(k, layers[j], dp, dq, low, 32), s4_send.at[at], s4_recv.at[at], near[1 - k, d]
        )

    def step_begin(j):
        if j > 0:
            same(G.at[c, layers[j], x, y], z_send.at[0], z_recv.at[layers[j]], sibling).wait_recv()
        for d in DIRS:
            for k in CLASSES:
                go(first(j, k, d, 0))
        for k in CLASSES:
            go(first_far(j, k, 0))
        for d in DIRS:
            for k in CLASSES:
                go(second(j, k, 0, d, 0))

    def step_middle(j):
        for dp in (-1, 1):
            for d in DIRS:
                for k in CLASSES:
                    if d == 1:
                        first(j, k, -dp, dp).wait_recv()
                    go(second(j, k, dp, d, 0))
        for d in DIRS:
            for k in CLASSES:
                if d == 1:
                    first_far(j, k, 2).wait_recv()
                go(second(j, k, 2, d, 0))

    def step_end(j):
        for dp in (0, -1, 1, 2):
            for d in DIRS:
                for k in CLASSES:
                    second(j, k, dp, d, -d).wait_recv()
                    go(second_far(j, k, dp, d, -d))

    def to_sibling(ref, at):
        return same(ref, sib_send.at[at], sib_recv.at[at], sibling)

    def last_part(core, k, dp):
        if k == 0:
            return G.at[core, layers[3], xs[dp], :, pl.ds(0, 64)]
        return G.at[core, layers[3], :, ys[dp], pl.ds(64, 64)]

    def step_finish(j):
        for dp in (0, -1, 1, 2):
            for k in CLASSES:
                for d in DIRS:
                    second_far(j, k, dp, d, 2).wait_recv()
                if j == 3:
                    go(to_sibling(last_part(c, k, dp), 3 + 4 * k + PIECE_AT[dp]))
        if j < 3:
            go(to_sibling(G.at[c, layers[j]], j))

    mine = G.at[c, zl, x, y]
    for j, mate in enumerate(z_mates):
        go(same(mine, z_send.at[j], z_recv.at[zl], mate))

    step_begin(0)

    loads[2].wait()
    feat_t[rep] = (inv * feat_v[...].astype(F32)).T.astype(BF16)

    loads[3].wait()
    count = count_ref[0, 0]

    def spread(i, carry):
        for n in range(4):
            tile = tiles_v[i * 4 + n]
            live = i * 4 + n < count
            at = rows_ref[0, i * 4 + n]
            for r in range(4):
                stacked[r, i, :, pl.ds(n * 128, 128)] = jnp.where(
                    jnp.logical_and(live, at == r), tile, jnp.zeros_like(tile)
                )
        return carry

    lax.fori_loop(0, SLOTS // 4, spread, 0)

    def step_stage(n):
        if n == 0:
            pl.semaphore_wait(ring1, 2)
            signal(ring2, ring(2))
            signal(ring2, ring(-2))
        elif n == 1:
            pl.semaphore_wait(ring2, 2)
            signal(ring3, ring(4))
            signal(ring3, ring(-4))
        else:
            pl.semaphore_wait(ring3, 2)
            for j, mate in enumerate(rep_mates):
                go(same(feat_t.at[rep], feat_send.at[j], feat_recv.at[rep], mate))

    steps = {
        "begin": step_begin, "middle": step_middle, "end": step_end, "finish": step_finish,
        "stage": step_stage,
    }
    for name, j in STEPS[1:]:
        steps[name](j)
    for j in range(3):
        to_sibling(G.at[1 - c, layers[j]], j).wait_recv()
    for dp in (0, -1, 1, 2):
        for k in CLASSES:
            to_sibling(last_part(1 - c, k, dp), 3 + 4 * k + PIECE_AT[dp]).wait_recv()

    def block(s):
        col = cols_ref[0, s]
        return G[col % 2, col // 32, (col // 8) % 4, (col // 2) % 4]

    def multiply(r):
        def add(i, acc):
            right = jnp.concatenate([block(i * 4 + n) for n in range(4)], axis=0)
            return acc + jnp.dot(stacked[r, i], right, preferred_element_type=F32)

        return lax.fori_loop(0, SLOTS // 4, add, jnp.zeros((128, 256), F32))

    gather_sends = list(sends)
    sends.clear()
    for j in (2, 1, 3):
        to = (rep + j) % 4
        part16[to] = multiply(to).astype(BF16)
        go(copy(part16.at[to], part_in.at[rep], part_send.at[j - 1], part_recv.at[rep], (row, to)))
    total[...] = multiply(rep)
    part16[rep] = total[...].astype(BF16)

    for j in (1, 2, 3):
        other = (rep + j) % 4
        same(feat_t.at[other], feat_send.at[0], feat_recv.at[other], sibling).wait_recv()
    term16 = jnp.dot(
        jnp.concatenate([feat_t[r] for r in range(4)], axis=1),
        jnp.concatenate([part16[r] for r in range(4)], axis=0),
        preferred_element_type=F32,
    ).astype(BF16)
    w16[0:16] = term16[:, 0:128].reshape(16, 16, 128)
    w16[16:32] = term16[:, 128:256].reshape(16, 16, 128)

    def wait_all(ref, count, sem):
        part = ref.at[pl.ds(0, count)]
        pltpu.make_async_copy(part, part, sem).wait()

    for j in range(1, 32):
        to = (layer_at + j) % 32
        copy(w16.at[to], w_in1.at[layer_at], w1_send, w1_recv, (zl * 32 + to, rep)).start()
    w_in1[layer_at] = w16[layer_at]
    for cp in gather_sends:
        cp.wait_send()
    wait_all(w_in1, 31, w1_recv)
    w_in2[z_at] = jnp.sum(w_in1[...].astype(F32), axis=0).astype(BF16)
    for j in range(1, 16):
        copy(w_in2.at[z_at], w_in2.at[z_at], w2_send, w2_recv, ring(j)).start()
    wait_all(w16, 31, w1_send)
    wait_all(w_in2, 15, w2_recv)
    w_in3[layer_at] = jnp.sum(w_in2[...].astype(F32), axis=0).astype(BF16)
    for j in range(1, 32):
        to = (layer_at + j) % 32
        copy(w_in3.at[layer_at], w_in3.at[layer_at], w3_send, w3_recv, (zl * 32 + to, rep)).start()

    for j in (1, 2, 3):
        at = (rep + j) % 4
        copy(part16.at[0], part_in.at[at], part_send.at[0], part_recv.at[at], sibling).wait_recv()
    agg = total[...]
    for j in (1, 2, 3):
        agg += part_in[(rep + j) % 4].astype(F32)
    loads[4].wait()
    gf_out[...] = lax.dot_general(
        (inv * agg).astype(BF16), weight_v[...], (((1,), (1,)), ((), ())),
        preferred_element_type=F32,
    ).astype(BF16)
    for cp in sends:
        cp.wait_send()
    wait_all(w_in2, 15, w2_send)

    wait_all(w_in3, 31, w3_recv)
    gw_out[:, 0:128] = w_in3[0:16].astype(F32).reshape(256, 128)
    gw_out[:, 128:256] = w_in3[16:32].astype(F32).reshape(256, 128)
    wait_all(w_in3, 31, w3_send)


def _power(zl):
    return 1 + (zl >= 1) * 63 + (zl >= 2) * (64 * 63) + (zl >= 3) * (64 * 64 * 63)


def per_device(
    grad_out, pre_act, features, weight, tile_values, tile_rows, tile_cols, tile_count, degrees
):
    dma = pltpu.SemaphoreType.DMA
    regular = pltpu.SemaphoreType.REGULAR
    vmem = pltpu.VMEM
    any_spec = pl.BlockSpec(memory_space=pl.ANY)
    smem_spec = pl.BlockSpec(memory_space=pltpu.SMEM)
    vmem_spec = pl.BlockSpec(memory_space=pltpu.VMEM)
    return pl.pallas_call(
        kernel,
        out_shape=(
            jax.ShapeDtypeStruct((128, 256), BF16),
            jax.ShapeDtypeStruct((256, 256), F32),
        ),
        in_specs=[any_spec] * 5 + [smem_spec] * 3 + [vmem_spec],
        out_specs=(vmem_spec, vmem_spec),
        scratch_shapes=[
            vmem((2, 4, 4, 4, 128, 256), BF16),
            vmem((128, 256), BF16),
            vmem((128, 256), BF16),
            vmem((128, 256), BF16),
            vmem((256, 256), BF16),
            vmem((SLOTS, 128, 128), BF16),
            vmem((4, SLOTS // 4, 128, 512), BF16),
            vmem((128, 256), F32),
            vmem((4, 256, 128), BF16),
            vmem((4, 128, 256), BF16),
            vmem((4, 128, 256), BF16),
            vmem((32, 16, 128), BF16),
            vmem((32, 16, 128), BF16),
            vmem((16, 16, 128), BF16),
            vmem((32, 16, 128), BF16),
            dma((5,)),
            dma((3,)), dma((4,)),
            dma((4, 2, 2)), dma((4, 2, 2)), dma((4, 2)), dma((4, 2)),
            dma((4, 2, 4, 2)), dma((4, 2, 4, 2)), dma((4, 2, 4, 2)), dma((4, 2, 4, 2)),
            dma((11,)), dma((11,)),
            dma((3,)), dma((4,)),
            dma((3,)), dma((4,)),
            dma, dma, dma, dma, dma, dma,
            regular, regular, regular,
        ],
        compiler_params=pltpu.CompilerParams(
            collective_id=0, has_side_effects=True, vmem_limit_bytes=62 * 2**20
        ),
    )(
        grad_out, pre_act, features, weight, tile_values[0, 0],
        tile_rows.reshape(1, SLOTS), tile_cols.reshape(1, SLOTS), tile_count,
        degrees.reshape(1, 128),
    )


def solution(mesh):
    in_specs = (
        P(("row", "rep"), None),
        P(("row", "rep"), None),
        P(("row", "rep"), None),
        P(),
        P("row", "rep", None, None, None),
        P("row", "rep", None),
        P("row", "rep", None),
        P("row", "rep"),
        P(("row", "rep")),
    )
    out_specs = (P(("row", "rep"), None), P())
    return jax.shard_map(
        per_device, mesh=mesh, in_specs=in_specs, out_specs=out_specs, check_vma=False
    )
```

```python
import jax
import jax.numpy as jnp
from jax import lax
from jax.experimental import pallas as pl
from jax.experimental.pallas import tpu as pltpu
from jax.sharding import PartitionSpec as P

MESH = pl.DeviceIdType.MESH
BF16 = jnp.bfloat16
F32 = jnp.float32
SLOTS = 48
EARLY = 0
DIRS = (1, -1)
CLASSES = (0, 1)
DIR_AT = {1: 0, -1: 1}
PIECE_AT = {0: 0, -1: 1, 1: 2, 2: 3}
LAYER_ORDER = [[1, 2, 3], [0, 2, 3], [3, 1, 0], [2, 1, 0]]
LAYER_CODE = sum(
    LAYER_ORDER[z][j] * 4 ** (z * 3 + j) for z in range(4) for j in range(3)
)
STEPS = (
    ("begin", 0), ("stage", 0), ("middle", 0), ("begin", 1), ("stage", 1), ("begin", 2), ("middle", 1),
    ("begin", 3), ("stage", 2), ("middle", 2), ("end", 0), ("middle", 3), ("end", 1), ("finish", 0),
    ("end", 2), ("finish", 1), ("end", 3), ("finish", 2), ("finish", 3),
)


def kernel(
    grad_hbm, pre_hbm, feat_hbm, weight_hbm, tiles_hbm, rows_ref, cols_ref, count_ref,
    degrees_ref, gf_out, gw_out,
    G, grad_v, pre_v, feat_v, weight_v, tiles_v, stacked, picked, total, feat_t, part16, part_in,
    w16, w_in1, w_in2, w_in3,
    load_sem, z_send, z_recv, s1_send, s1_recv, s2_send, s2_recv, s3_send, s3_recv,
    s4_send, s4_recv, sib_send, sib_recv, feat_send, feat_recv, part_send, part_recv,
    w1_send, w1_recv, w2_send, w2_recv, w3_send, w3_recv, ring1, ring2, ring3,
):
    row = lax.axis_index("row")
    rep = lax.axis_index("rep")
    c = row % 2
    y = (row // 2) % 4
    x = (row // 8) % 4
    zl = row // 32
    layer_at = row % 32

    def dev(at_z, at_x, at_y, at_c):
        return (((at_z * 4 + at_x) * 4 + at_y) * 2 + at_c, rep)

    xs = {0: x, 1: (x + 1) % 4, 2: (x + 2) % 4, -1: (x + 3) % 4}
    ys = {0: y, 1: (y + 1) % 4, 2: (y + 2) % 4, -1: (y + 3) % 4}
    near = {
        (0, 1): dev(zl, xs[1], y, c),
        (0, -1): dev(zl, xs[-1], y, c),
        (1, 1): dev(zl, x, ys[1], c),
        (1, -1): dev(zl, x, ys[-1], c),
    }
    sibling = dev(zl, x, y, 1 - c)
    z_mates = [dev((zl + j) % 4, x, y, c) for j in (1, 2, 3)]
    rep_mates = [(row, (rep + j) % 4) for j in (1, 2, 3)]
    far = {0: dev(zl, xs[2], y, c), 1: dev(zl, x, ys[2], c)}
    z_at = rep * 4 + zl

    def ring(step):
        at = (z_at + step + 16) % 16
        return ((at % 4) * 32 + layer_at, at // 4)

    def signal(sem, to):
        pl.semaphore_signal(sem, inc=1, device_id=to, device_id_type=MESH)


    loads = [
        pltpu.make_async_copy(src, dst, load_sem.at[i])
        for i, (src, dst) in enumerate(
            [
                (grad_hbm, grad_v),
                (pre_hbm, pre_v),
                (feat_hbm, feat_v),
                (tiles_hbm, tiles_v),
                (weight_hbm, weight_v),
            ]
        )
    ]
    for load in loads:
        load.start()

    barrier = pltpu.get_barrier_semaphore()
    peers = list(near.values()) + list(far.values()) + [sibling] + z_mates + [ring(1), ring(-1)]
    for peer in peers:
        signal(barrier, peer)

    inv_row = lax.rsqrt(degrees_ref[...].astype(F32))
    inv_half = jnp.broadcast_to(inv_row, (128, 128)).T
    inv = jnp.concatenate([inv_half, inv_half], axis=1)

    loads[0].wait()
    loads[1].wait()
    pre = pre_v[...].astype(F32)
    gate = jax.nn.sigmoid(pre)
    grad_pre = grad_v[...].astype(F32) * gate * (1.0 + pre * (1.0 - gate))
    G[c, zl, x, y] = (inv * grad_pre).astype(BF16)

    pl.semaphore_wait(barrier, len(peers))
    signal(ring1, ring(1))
    signal(ring1, ring(-1))

    sends = []

    def copy(src, dst, send_sem, recv_sem, to):
        return pltpu.make_async_remote_copy(
            src_ref=src,
            dst_ref=dst,
            send_sem=send_sem,
            recv_sem=recv_sem,
            device_id=to,
            device_id_type=MESH,
        )

    def same(ref, send_sem, recv_sem, to):
        return copy(ref, ref, send_sem, recv_sem, to)

    def go(cp):
        cp.start()
        sends.append(cp)

    layers = [zl] + [(LAYER_CODE // 4 ** j // _power(zl)) % 4 for j in range(3)]

    def piece(k, layer, dp, dq, low, size):
        dx, dy = (dp, dq) if k == 0 else (dq, dp)
        return G.at[c, layer, xs[dx], ys[dy], pl.ds(k * 64 + low, size)]

    def first(j, k, d, dp):
        at = (j, k, DIR_AT[d])
        return same(piece(k, layers[j], dp, 0, 0, 64), s1_send.at[at], s1_recv.at[at], near[k, d])

    def first_far(j, k, dp):
        at = (j, k)
        return same(piece(k, layers[j], dp, 0, 0, 64), s2_send.at[at], s2_recv.at[at], far[k])

    def second(j, k, dp, d, dq):
        at = (j, k, PIECE_AT[dp], DIR_AT[d])
        return same(
            piece(k, layers[j], dp, dq, 0, 64), s3_send.at[at], s3_recv.at[at], near[1 - k, d]
        )

    def second_far(j, k, dp, d, dq):
        at = (j, k, PIECE_AT[dp], DIR_AT[d])
        low = 0 if d == 1 else 32
        return same(
            piece(k, layers[j], dp, dq, low, 32), s4_send.at[at], s4_recv.at[at], near[1 - k, d]
        )

    def step_begin(j):
        if j > 0:
            same(G.at[c, layers[j], x, y], z_send.at[0], z_recv.at[layers[j]], sibling).wait_recv()
        for d in DIRS:
            for k in CLASSES:
                go(first(j, k, d, 0))
        for k in CLASSES:
            go(first_far(j, k, 0))
        for d in DIRS:
            for k in CLASSES:
                go(second(j, k, 0, d, 0))

    def step_middle(j):
        for dp in (-1, 1):
            for d in DIRS:
                for k in CLASSES:
                    if d == 1:
                        first(j, k, -dp, dp).wait_recv()
                    go(second(j, k, dp, d, 0))
        for d in DIRS:
            for k in CLASSES:
                if d == 1:
                    first_far(j, k, 2).wait_recv()
                go(second(j, k, 2, d, 0))
        for k in CLASSES:
            go(to_sibling(c, j, k, 0))

    def step_end(j):
        for dp in (0, -1, 1, 2):
            for d in DIRS:
                for k in CLASSES:
                    second(j, k, dp, d, -d).wait_recv()
                    go(second_far(j, k, dp, d, -d))
        for d in DIRS:
            for k in CLASSES:
                go(to_sibling(c, j, k, d))

    def to_sibling(core, j, k, dq):
        if k == 0:
            ref = G.at[core, layers[j], :, ys[dq], pl.ds(0, 64)]
        else:
            ref = G.at[core, layers[j], xs[dq], :, pl.ds(64, 64)]
        at = (j, k, PIECE_AT[dq])
        return same(ref, sib_send.at[at], sib_recv.at[at], sibling)

    def step_finish(j):
        for k in CLASSES:
            for dp in (0, -1, 1, 2):
                for d in DIRS:
                    second_far(j, k, dp, d, 2).wait_recv()
            go(to_sibling(c, j, k, 2))

    mine = G.at[c, zl, x, y]
    for j, mate in enumerate(z_mates):
        go(same(mine, z_send.at[j], z_recv.at[zl], mate))

    step_begin(0)

    loads[2].wait()
    feat_t[rep] = (inv * feat_v[...].astype(F32)).T.astype(BF16)

    loads[3].wait()
    count = count_ref[0, 0]

    def spread(s, carry):
        tile = tiles_v[s]
        live = s < count
        at = rows_ref[0, s]
        for r in range(4):
            stacked[r, :, pl.ds(pl.multiple_of(s * 128, 128), 128)] = jnp.where(
                jnp.logical_and(live, at == r), tile, jnp.zeros_like(tile)
            )
        return carry

    lax.fori_loop(0, SLOTS, spread, 0)

    def step_stage(n):
        if n == 0:
            pl.semaphore_wait(ring1, 2)
            signal(ring2, ring(2))
            signal(ring2, ring(-2))
        elif n == 1:
            pl.semaphore_wait(ring2, 2)
            signal(ring3, ring(4))
            signal(ring3, ring(-4))
        else:
            pl.semaphore_wait(ring3, 2)
            for j, mate in enumerate(rep_mates):
                go(same(feat_t.at[rep], feat_send.at[j], feat_recv.at[rep], mate))

    steps = {
        "begin": step_begin, "middle": step_middle, "end": step_end, "finish": step_finish,
        "stage": step_stage,
    }
    for name, j in STEPS[1:]:
        steps[name](j)
    for j in range(4):
        for k in CLASSES:
            for dq in (0, -1, 1, 2):
                to_sibling(1 - c, j, k, dq).wait_recv()

    for s in range(SLOTS):
        col = cols_ref[0, s]
        picked[pl.ds(s * 128, 128), :] = G[col % 2, col // 32, (col // 8) % 4, (col // 2) % 4]

    def multiply(r):
        return jnp.dot(stacked[r], picked[...], preferred_element_type=F32)

    gather_sends = list(sends)
    sends.clear()
    for j in (2, 1, 3):
        to = (rep + j) % 4
        part16[to] = multiply(to).astype(BF16)
        go(copy(part16.at[to], part_in.at[rep], part_send.at[j - 1], part_recv.at[rep], (row, to)))
    total[...] = multiply(rep)
    part16[rep] = total[...].astype(BF16)

    for j in (1, 2, 3):
        other = (rep + j) % 4
        same(feat_t.at[other], feat_send.at[0], feat_recv.at[other], sibling).wait_recv()
    term16 = jnp.dot(
        jnp.concatenate([feat_t[r] for r in range(4)], axis=1),
        jnp.concatenate([part16[r] for r in range(4)], axis=0),
        preferred_element_type=F32,
    ).astype(BF16)
    w16[0:16] = term16[:, 0:128].reshape(16, 16, 128)
    w16[16:32] = term16[:, 128:256].reshape(16, 16, 128)

    def wait_all(ref, count, sem):
        part = ref.at[pl.ds(0, count)]
        pltpu.make_async_copy(part, part, sem).wait()

    for j in range(1, 32):
        to = (layer_at + j) % 32
        copy(w16.at[to], w_in1.at[layer_at], w1_send, w1_recv, (zl * 32 + to, rep)).start()
    w_in1[layer_at] = w16[layer_at]
    for cp in gather_sends[:EARLY]:
        cp.wait_send()
    wait_all(w_in1, 31, w1_recv)
    w_in2[z_at] = jnp.sum(w_in1[...].astype(F32), axis=0).astype(BF16)
    for j in range(1, 16):
        copy(w_in2.at[z_at], w_in2.at[z_at], w2_send, w2_recv, ring(j)).start()
    wait_all(w16, 31, w1_send)
    for cp in gather_sends[EARLY:]:
        cp.wait_send()
    wait_all(w_in2, 15, w2_recv)
    w_in3[layer_at] = jnp.sum(w_in2[...].astype(F32), axis=0).astype(BF16)
    for j in range(1, 32):
        to = (layer_at + j) % 32
        copy(w_in3.at[layer_at], w_in3.at[layer_at], w3_send, w3_recv, (zl * 32 + to, rep)).start()

    for j in (1, 2, 3):
        at = (rep + j) % 4
        copy(part16.at[0], part_in.at[at], part_send.at[0], part_recv.at[at], sibling).wait_recv()
    agg = total[...]
    for j in (1, 2, 3):
        agg += part_in[(rep + j) % 4].astype(F32)
    loads[4].wait()
    gf_out[...] = lax.dot_general(
        (inv * agg).astype(BF16), weight_v[...], (((1,), (1,)), ((), ())),
        preferred_element_type=F32,
    ).astype(BF16)
    for cp in sends:
        cp.wait_send()
    wait_all(w_in2, 15, w2_send)

    wait_all(w_in3, 31, w3_recv)
    gw_out[:, 0:128] = w_in3[0:16].astype(F32).reshape(256, 128)
    gw_out[:, 128:256] = w_in3[16:32].astype(F32).reshape(256, 128)
    wait_all(w_in3, 31, w3_send)


def _power(zl):
    return 1 + (zl >= 1) * 63 + (zl >= 2) * (64 * 63) + (zl >= 3) * (64 * 64 * 63)


def per_device(
    grad_out, pre_act, features, weight, tile_values, tile_rows, tile_cols, tile_count, degrees
):
    dma = pltpu.SemaphoreType.DMA
    regular = pltpu.SemaphoreType.REGULAR
    vmem = pltpu.VMEM
    any_spec = pl.BlockSpec(memory_space=pl.ANY)
    smem_spec = pl.BlockSpec(memory_space=pltpu.SMEM)
    vmem_spec = pl.BlockSpec(memory_space=pltpu.VMEM)
    return pl.pallas_call(
        kernel,
        out_shape=(
            jax.ShapeDtypeStruct((128, 256), BF16),
            jax.ShapeDtypeStruct((256, 256), F32),
        ),
        in_specs=[any_spec] * 5 + [smem_spec] * 3 + [vmem_spec],
        out_specs=(vmem_spec, vmem_spec),
        scratch_shapes=[
            vmem((2, 4, 4, 4, 128, 256), BF16),
            vmem((128, 256), BF16),
            vmem((128, 256), BF16),
            vmem((128, 256), BF16),
            vmem((256, 256), BF16),
            vmem((SLOTS, 128, 128), BF16),
            vmem((4, 128, SLOTS * 128), BF16),
            vmem((SLOTS * 128, 256), BF16),
            vmem((128, 256), F32),
            vmem((4, 256, 128), BF16),
            vmem((4, 128, 256), BF16),
            vmem((4, 128, 256), BF16),
            vmem((32, 16, 128), BF16),
            vmem((32, 16, 128), BF16),
            vmem((16, 16, 128), BF16),
            vmem((32, 16, 128), BF16),
            dma((5,)),
            dma((3,)), dma((4,)),
            dma((4, 2, 2)), dma((4, 2, 2)), dma((4, 2)), dma((4, 2)),
            dma((4, 2, 4, 2)), dma((4, 2, 4, 2)), dma((4, 2, 4, 2)), dma((4, 2, 4, 2)),
            dma((4, 2, 4)), dma((4, 2, 4)),
            dma((3,)), dma((4,)),
            dma((3,)), dma((4,)),
            dma, dma, dma, dma, dma, dma,
            regular, regular, regular,
        ],
        compiler_params=pltpu.CompilerParams(
            collective_id=0, has_side_effects=True, vmem_limit_bytes=62 * 2**20
        ),
    )(
        grad_out, pre_act, features, weight, tile_values[0, 0],
        tile_rows.reshape(1, SLOTS), tile_cols.reshape(1, SLOTS), tile_count,
        degrees.reshape(1, 128),
    )


def solution(mesh):
    in_specs = (
        P(("row", "rep"), None),
        P(("row", "rep"), None),
        P(("row", "rep"), None),
        P(),
        P("row", "rep", None, None, None),
        P("row", "rep", None),
        P("row", "rep", None),
        P("row", "rep"),
        P(("row", "rep")),
    )
    out_specs = (P(("row", "rep"), None), P())
    return jax.shard_map(
        per_device, mesh=mesh, in_specs=in_specs, out_specs=out_specs, check_vma=False
    )
```

```python
import jax
import jax.numpy as jnp
from jax import lax
from jax.experimental import pallas as pl
from jax.experimental.pallas import tpu as pltpu
from jax.sharding import PartitionSpec as P

MESH = pl.DeviceIdType.MESH
BF16 = jnp.bfloat16
F32 = jnp.float32
SLOTS = 48
LAYER_OFFSETS = sorted(
    [(dx, dy, dc) for dx in (2, 1, -1, 0) for dy in (2, 1, -1, 0) for dc in (0, 1)],
    key=lambda at: -(abs(at[0]) + abs(at[1]) + at[2] / 2),
)[:-1]
RING_STEPS = sorted(range(1, 16), key=lambda j: -min(j, 16 - j))
DIRS = (1, -1)
CLASSES = (0, 1)
DIR_AT = {1: 0, -1: 1}
PIECE_AT = {0: 0, -1: 1, 1: 2, 2: 3}
LAYER_ORDER = [[1, 2, 3], [0, 2, 3], [3, 1, 0], [2, 1, 0]]
LAYER_CODE = sum(
    LAYER_ORDER[z][j] * 4 ** (z * 3 + j) for z in range(4) for j in range(3)
)
STEPS = (
    ("begin", 0), ("stage", 0), ("middle", 0), ("begin", 1), ("stage", 1), ("begin", 2), ("middle", 1),
    ("begin", 3), ("stage", 2), ("middle", 2), ("end", 0), ("middle", 3), ("end", 1), ("finish", 0),
    ("end", 2), ("finish", 1), ("end", 3), ("finish", 2), ("finish", 3),
)


def kernel(
    grad_hbm, pre_hbm, feat_hbm, weight_hbm, tiles_hbm, rows_hbm, cols_hbm, count_hbm,
    degrees_hbm, gf_out, gw_out,
    rows_ref, cols_ref, count_ref, degrees_ref, G, grad_v, pre_v, feat_v, weight_v, tiles_v, stacked, picked, total, feat_t, part16, part_in,
    w16, w_in1, w_in2, w_in3,
    load_sem, z_send, z_recv, s1_send, s1_recv, s2_send, s2_recv, s3_send, s3_recv,
    s4_send, s4_recv, sib_send, sib_recv, feat_send, feat_recv, part_send, part_recv,
    w1_send, w1_recv, w2_send, w2_recv, w3_send, w3_recv, ring1, ring2, ring3,
):
    row = lax.axis_index("row")
    rep = lax.axis_index("rep")
    c = row % 2
    y = (row // 2) % 4
    x = (row // 8) % 4
    zl = row // 32
    layer_at = row % 32

    def dev(at_z, at_x, at_y, at_c):
        return (((at_z * 4 + at_x) * 4 + at_y) * 2 + at_c, rep)

    xs = {0: x, 1: (x + 1) % 4, 2: (x + 2) % 4, -1: (x + 3) % 4}
    ys = {0: y, 1: (y + 1) % 4, 2: (y + 2) % 4, -1: (y + 3) % 4}
    near = {
        (0, 1): dev(zl, xs[1], y, c),
        (0, -1): dev(zl, xs[-1], y, c),
        (1, 1): dev(zl, x, ys[1], c),
        (1, -1): dev(zl, x, ys[-1], c),
    }
    sibling = dev(zl, x, y, 1 - c)
    z_mates = [dev((zl + j) % 4, x, y, c) for j in (1, 2, 3)]
    rep_mates = [(row, (rep + j) % 4) for j in (1, 2, 3)]
    far = {0: dev(zl, xs[2], y, c), 1: dev(zl, x, ys[2], c)}
    z_at = rep * 4 + zl

    def ring(step):
        at = (z_at + step + 16) % 16
        return ((at % 4) * 32 + layer_at, at // 4)

    def signal(sem, to):
        pl.semaphore_signal(sem, inc=1, device_id=to, device_id_type=MESH)


    loads = [
        pltpu.make_async_copy(src, dst, load_sem.at[i])
        for i, (src, dst) in enumerate(
            [
                (grad_hbm, grad_v),
                (pre_hbm, pre_v),
                (feat_hbm, feat_v),
                (tiles_hbm, tiles_v),
                (weight_hbm, weight_v),
                (degrees_hbm, degrees_ref),
                (rows_hbm, rows_ref),
                (cols_hbm, cols_ref),
                (count_hbm, count_ref),
            ]
        )
    ]
    for load in loads:
        load.start()

    barrier = pltpu.get_barrier_semaphore()
    peers = list(near.values()) + list(far.values()) + [sibling] + z_mates + [ring(1), ring(-1)]
    for peer in peers:
        signal(barrier, peer)

    loads[5].wait()
    inv_row = lax.rsqrt(degrees_ref[...].astype(F32))
    inv_half = jnp.broadcast_to(inv_row, (128, 128)).T
    inv = jnp.concatenate([inv_half, inv_half], axis=1)

    loads[0].wait()
    loads[1].wait()
    pre = pre_v[...].astype(F32)
    gate = jax.nn.sigmoid(pre)
    grad_pre = grad_v[...].astype(F32) * gate * (1.0 + pre * (1.0 - gate))
    G[c, zl, x, y] = (inv * grad_pre).astype(BF16)

    pl.semaphore_wait(barrier, len(peers))
    signal(ring1, ring(1))
    signal(ring1, ring(-1))

    sends = []

    def copy(src, dst, send_sem, recv_sem, to):
        return pltpu.make_async_remote_copy(
            src_ref=src,
            dst_ref=dst,
            send_sem=send_sem,
            recv_sem=recv_sem,
            device_id=to,
            device_id_type=MESH,
        )

    def same(ref, send_sem, recv_sem, to):
        return copy(ref, ref, send_sem, recv_sem, to)

    def go(cp):
        cp.start()
        sends.append(cp)

    layers = [zl] + [(LAYER_CODE // 4 ** j // _power(zl)) % 4 for j in range(3)]

    def piece(k, layer, dp, dq, low, size):
        dx, dy = (dp, dq) if k == 0 else (dq, dp)
        return G.at[c, layer, xs[dx], ys[dy], pl.ds(k * 64 + low, size)]

    def first(j, k, d, dp):
        at = (j, k, DIR_AT[d])
        return same(piece(k, layers[j], dp, 0, 0, 64), s1_send.at[at], s1_recv.at[at], near[k, d])

    def first_far(j, k, dp):
        at = (j, k)
        return same(piece(k, layers[j], dp, 0, 0, 64), s2_send.at[at], s2_recv.at[at], far[k])

    def second(j, k, dp, d, dq):
        at = (j, k, PIECE_AT[dp], DIR_AT[d])
        return same(
            piece(k, layers[j], dp, dq, 0, 64), s3_send.at[at], s3_recv.at[at], near[1 - k, d]
        )

    def second_far(j, k, dp, d, dq):
        at = (j, k, PIECE_AT[dp], DIR_AT[d])
        low = 0 if d == 1 else 32
        return same(
            piece(k, layers[j], dp, dq, low, 32), s4_send.at[at], s4_recv.at[at], near[1 - k, d]
        )

    def step_begin(j):
        if j > 0:
            same(G.at[c, layers[j], x, y], z_send.at[0], z_recv.at[layers[j]], sibling).wait_recv()
        for d in DIRS:
            for k in CLASSES:
                go(first(j, k, d, 0))
        for k in CLASSES:
            go(first_far(j, k, 0))
        for d in DIRS:
            for k in CLASSES:
                go(second(j, k, 0, d, 0))

    def step_middle(j):
        for dp in (-1, 1):
            for d in DIRS:
                for k in CLASSES:
                    if d == 1:
                        first(j, k, -dp, dp).wait_recv()
                    go(second(j, k, dp, d, 0))
        for d in DIRS:
            for k in CLASSES:
                if d == 1:
                    first_far(j, k, 2).wait_recv()
                go(second(j, k, 2, d, 0))
        for k in CLASSES:
            go(to_sibling(c, j, k, 0))

    def step_end(j):
        for dp in (0, -1, 1, 2):
            for d in DIRS:
                for k in CLASSES:
                    second(j, k, dp, d, -d).wait_recv()
                    go(second_far(j, k, dp, d, -d))
        for d in DIRS:
            for k in CLASSES:
                go(to_sibling(c, j, k, d))

    def to_sibling(core, j, k, dq):
        if k == 0:
            ref = G.at[core, layers[j], :, ys[dq], pl.ds(0, 64)]
        else:
            ref = G.at[core, layers[j], xs[dq], :, pl.ds(64, 64)]
        at = (j, k, PIECE_AT[dq])
        return same(ref, sib_send.at[at], sib_recv.at[at], sibling)

    def step_finish(j):
        for k in CLASSES:
            for dp in (0, -1, 1, 2):
                for d in DIRS:
                    second_far(j, k, dp, d, 2).wait_recv()
            go(to_sibling(c, j, k, 2))

    mine = G.at[c, zl, x, y]
    for j, mate in enumerate(z_mates):
        go(same(mine, z_send.at[j], z_recv.at[zl], mate))

    step_begin(0)

    loads[2].wait()
    feat_t[rep] = (inv * feat_v[...].astype(F32)).T.astype(BF16)

    loads[3].wait()
    for load in loads[6:]:
        load.wait()
    count = count_ref[0, 0]

    def spread(s, carry):
        tile = tiles_v[s]
        live = s < count
        at = rows_ref[0, s]
        for r in range(4):
            stacked[r, :, pl.ds(pl.multiple_of(s * 128, 128), 128)] = jnp.where(
                jnp.logical_and(live, at == r), tile, jnp.zeros_like(tile)
            )
        return carry

    lax.fori_loop(0, SLOTS, spread, 0)

    def step_stage(n):
        if n == 0:
            pl.semaphore_wait(ring1, 2)
            signal(ring2, ring(2))
            signal(ring2, ring(-2))
        elif n == 1:
            pl.semaphore_wait(ring2, 2)
            signal(ring3, ring(4))
            signal(ring3, ring(-4))
        else:
            pl.semaphore_wait(ring3, 2)
            for j, mate in enumerate(rep_mates):
                go(same(feat_t.at[rep], feat_send.at[j], feat_recv.at[rep], mate))

    steps = {
        "begin": step_begin, "middle": step_middle, "end": step_end, "finish": step_finish,
        "stage": step_stage,
    }
    for name, j in STEPS[1:]:
        steps[name](j)
    for j in range(4):
        for k in CLASSES:
            for dq in (0, -1, 1, 2):
                to_sibling(1 - c, j, k, dq).wait_recv()

    for s in range(SLOTS):
        col = cols_ref[0, s]
        picked[pl.ds(s * 128, 128), :] = G[col % 2, col // 32, (col // 8) % 4, (col // 2) % 4]

    def multiply(r):
        return jnp.dot(stacked[r], picked[...], preferred_element_type=F32)

    def part_to(j):
        to = (rep + j) % 4
        return copy(part16.at[to], part_in.at[rep], part_send.at[j - 1], part_recv.at[rep], (row, to))

    gather_sends = list(sends)
    sends.clear()
    for j in (2, 1, 3):
        to = (rep + j) % 4
        part16[to] = multiply(to).astype(BF16)
        if j != 2:
            go(part_to(j))
    total[...] = multiply(rep)
    part16[rep] = total[...].astype(BF16)

    for j in (1, 2, 3):
        other = (rep + j) % 4
        same(feat_t.at[other], feat_send.at[0], feat_recv.at[other], sibling).wait_recv()
    term16 = jnp.dot(
        jnp.concatenate([feat_t[r] for r in range(4)], axis=1),
        jnp.concatenate([part16[r] for r in range(4)], axis=0),
        preferred_element_type=F32,
    ).astype(BF16)
    w16[0:16] = term16[:, 0:128].reshape(16, 16, 128)
    w16[16:32] = term16[:, 128:256].reshape(16, 16, 128)

    def wait_all(ref, count, sem):
        part = ref.at[pl.ds(0, count)]
        pltpu.make_async_copy(part, part, sem).wait()

    layer_mates = [xs[dx] * 8 + ys[dy] * 2 + (1 - c if dc else c) for dx, dy, dc in LAYER_OFFSETS]
    for to in layer_mates:
        copy(w16.at[to], w_in1.at[layer_at], w1_send, w1_recv, (zl * 32 + to, rep)).start()
    w_in1[layer_at] = w16[layer_at]
    wait_all(w_in1, 31, w1_recv)
    w_in2[z_at] = jnp.sum(w_in1[...].astype(F32), axis=0).astype(BF16)
    for j in RING_STEPS:
        copy(w_in2.at[z_at], w_in2.at[z_at], w2_send, w2_recv, ring(j)).start()
    go(part_to(2))
    wait_all(w16, 31, w1_send)
    for cp in gather_sends:
        cp.wait_send()
    wait_all(w_in2, 15, w2_recv)
    w_in3[layer_at] = jnp.sum(w_in2[...].astype(F32), axis=0).astype(BF16)
    for to in layer_mates:
        copy(w_in3.at[layer_at], w_in3.at[layer_at], w3_send, w3_recv, (zl * 32 + to, rep)).start()

    for j in (1, 2, 3):
        at = (rep + j) % 4
        copy(part16.at[0], part_in.at[at], part_send.at[0], part_recv.at[at], sibling).wait_recv()
    agg = total[...]
    for j in (1, 2, 3):
        agg += part_in[(rep + j) % 4].astype(F32)
    loads[4].wait()
    gf_out[...] = lax.dot_general(
        (inv * agg).astype(BF16), weight_v[...], (((1,), (1,)), ((), ())),
        preferred_element_type=F32,
    ).astype(BF16)
    for cp in sends:
        cp.wait_send()
    wait_all(w_in2, 15, w2_send)

    wait_all(w_in3, 31, w3_recv)
    gw_out[:, 0:128] = w_in3[0:16].astype(F32).reshape(256, 128)
    gw_out[:, 128:256] = w_in3[16:32].astype(F32).reshape(256, 128)
    wait_all(w_in3, 31, w3_send)


def _power(zl):
    return 1 + (zl >= 1) * 63 + (zl >= 2) * (64 * 63) + (zl >= 3) * (64 * 64 * 63)


def per_device(
    grad_out, pre_act, features, weight, tile_values, tile_rows, tile_cols, tile_count, degrees
):
    dma = pltpu.SemaphoreType.DMA
    regular = pltpu.SemaphoreType.REGULAR
    vmem = pltpu.VMEM
    any_spec = pl.BlockSpec(memory_space=pl.ANY)
    vmem_spec = pl.BlockSpec(memory_space=pltpu.VMEM)
    return pl.pallas_call(
        kernel,
        out_shape=(
            jax.ShapeDtypeStruct((128, 256), BF16),
            jax.ShapeDtypeStruct((256, 256), F32),
        ),
        in_specs=[any_spec] * 9,
        out_specs=(vmem_spec, vmem_spec),
        scratch_shapes=[
            pltpu.SMEM((1, SLOTS), jnp.int32),
            pltpu.SMEM((1, SLOTS), jnp.int32),
            pltpu.SMEM((1, 1), jnp.int32),
            vmem((1, 128), jnp.int32),
            vmem((2, 4, 4, 4, 128, 256), BF16),
            vmem((128, 256), BF16),
            vmem((128, 256), BF16),
            vmem((128, 256), BF16),
            vmem((256, 256), BF16),
            vmem((SLOTS, 128, 128), BF16),
            vmem((4, 128, SLOTS * 128), BF16),
            vmem((SLOTS * 128, 256), BF16),
            vmem((128, 256), F32),
            vmem((4, 256, 128), BF16),
            vmem((4, 128, 256), BF16),
            vmem((4, 128, 256), BF16),
            vmem((32, 16, 128), BF16),
            vmem((32, 16, 128), BF16),
            vmem((16, 16, 128), BF16),
            vmem((32, 16, 128), BF16),
            dma((9,)),
            dma((3,)), dma((4,)),
            dma((4, 2, 2)), dma((4, 2, 2)), dma((4, 2)), dma((4, 2)),
            dma((4, 2, 4, 2)), dma((4, 2, 4, 2)), dma((4, 2, 4, 2)), dma((4, 2, 4, 2)),
            dma((4, 2, 4)), dma((4, 2, 4)),
            dma((3,)), dma((4,)),
            dma((3,)), dma((4,)),
            dma, dma, dma, dma, dma, dma,
            regular, regular, regular,
        ],
        compiler_params=pltpu.CompilerParams(
            collective_id=0, has_side_effects=True, vmem_limit_bytes=62 * 2**20
        ),
    )(
        grad_out, pre_act, features, weight, tile_values[0, 0],
        tile_rows.reshape(1, SLOTS), tile_cols.reshape(1, SLOTS), tile_count,
        degrees.reshape(1, 128),
    )


def solution(mesh):
    in_specs = (
        P(("row", "rep"), None),
        P(("row", "rep"), None),
        P(("row", "rep"), None),
        P(),
        P("row", "rep", None, None, None),
        P("row", "rep", None),
        P("row", "rep", None),
        P("row", "rep"),
        P(("row", "rep")),
    )
    out_specs = (P(("row", "rep"), None), P())
    return jax.shard_map(
        per_device, mesh=mesh, in_specs=in_specs, out_specs=out_specs, check_vma=False
    )
```

```python
import jax
import jax.numpy as jnp
from jax import lax
from jax.experimental import pallas as pl
from jax.experimental.pallas import tpu as pltpu
from jax.sharding import PartitionSpec as P

MESH = pl.DeviceIdType.MESH
BF16 = jnp.bfloat16
F32 = jnp.float32
SLOTS = 48
LAYER_OFFSETS = sorted(
    [(dx, dy, dc) for dx in (2, 1, -1, 0) for dy in (2, 1, -1, 0) for dc in (0, 1)],
    key=lambda at: -(abs(at[0]) + abs(at[1]) + at[2] / 2),
)[:-1]
RING_STEPS = sorted(range(1, 16), key=lambda j: -min(j, 16 - j))
DIRS = (1, -1)
CLASSES = (0, 1)
DIR_AT = {1: 0, -1: 1}
PIECE_AT = {0: 0, -1: 1, 1: 2, 2: 3}
LAYER_ORDER = [[1, 2, 3], [0, 2, 3], [3, 1, 0], [2, 1, 0]]
LAYER_CODE = sum(
    LAYER_ORDER[z][j] * 4 ** (z * 3 + j) for z in range(4) for j in range(3)
)
STEPS = (
    ("begin", 0), ("stage", 0), ("middle", 0), ("begin", 1), ("stage", 1), ("begin", 2), ("middle", 1),
    ("begin", 3), ("stage", 2), ("middle", 2), ("end", 0), ("middle", 3), ("end", 1), ("end", 2),
    ("finish", 0), ("end", 3), ("finish", 1), ("finish", 2), ("finish", 3),
)


def kernel(
    grad_hbm, pre_hbm, feat_hbm, weight_hbm, tiles_hbm, rows_hbm, cols_hbm, count_hbm,
    degrees_hbm, gf_out, gw_out,
    rows_ref, cols_ref, count_ref, degrees_ref, G, grad_v, pre_v, feat_v, weight_v, tiles_v, stacked, picked, total, feat_t, part16, part_in,
    w16, w_in1, w_in2, w_in3,
    load_sem, z_send, z_recv, s1_send, s1_recv, s2_send, s2_recv, s3_send, s3_recv,
    s4_send, s4_recv, sib_send, sib_recv, feat_send, feat_recv, part_send, part_recv,
    w1_send, w1_recv, w2_send, w2_recv, w3_send, w3_recv, ring1, ring2, ring3,
):
    row = lax.axis_index("row")
    rep = lax.axis_index("rep")
    c = row % 2
    y = (row // 2) % 4
    x = (row // 8) % 4
    zl = row // 32
    layer_at = row % 32

    def dev(at_z, at_x, at_y, at_c):
        return (((at_z * 4 + at_x) * 4 + at_y) * 2 + at_c, rep)

    xs = {0: x, 1: (x + 1) % 4, 2: (x + 2) % 4, -1: (x + 3) % 4}
    ys = {0: y, 1: (y + 1) % 4, 2: (y + 2) % 4, -1: (y + 3) % 4}
    near = {
        (0, 1): dev(zl, xs[1], y, c),
        (0, -1): dev(zl, xs[-1], y, c),
        (1, 1): dev(zl, x, ys[1], c),
        (1, -1): dev(zl, x, ys[-1], c),
    }
    sibling = dev(zl, x, y, 1 - c)
    z_mates = [dev((zl + j) % 4, x, y, c) for j in (1, 2, 3)]
    rep_mates = [(row, (rep + j) % 4) for j in (1, 2, 3)]
    far = {0: dev(zl, xs[2], y, c), 1: dev(zl, x, ys[2], c)}
    z_at = rep * 4 + zl

    def ring(step):
        at = (z_at + step + 16) % 16
        return ((at % 4) * 32 + layer_at, at // 4)

    def signal(sem, to):
        pl.semaphore_signal(sem, inc=1, device_id=to, device_id_type=MESH)


    loads = [
        pltpu.make_async_copy(src, dst, load_sem.at[i])
        for i, (src, dst) in enumerate(
            [
                (grad_hbm, grad_v),
                (pre_hbm, pre_v),
                (feat_hbm, feat_v),
                (tiles_hbm, tiles_v),
                (weight_hbm, weight_v),
                (degrees_hbm, degrees_ref),
                (rows_hbm, rows_ref),
                (cols_hbm, cols_ref),
                (count_hbm, count_ref),
            ]
        )
    ]
    for load in loads:
        load.start()

    barrier = pltpu.get_barrier_semaphore()
    peers = list(near.values()) + list(far.values()) + [sibling] + z_mates + [ring(1), ring(-1)]
    for peer in peers:
        signal(barrier, peer)

    loads[5].wait()
    inv_row = lax.rsqrt(degrees_ref[...].astype(F32))
    inv_half = jnp.broadcast_to(inv_row, (128, 128)).T
    inv = jnp.concatenate([inv_half, inv_half], axis=1)

    loads[0].wait()
    loads[1].wait()
    pre = pre_v[...].astype(F32)
    gate = jax.nn.sigmoid(pre)
    grad_pre = grad_v[...].astype(F32) * gate * (1.0 + pre * (1.0 - gate))
    G[c, zl, x, y] = (inv * grad_pre).astype(BF16)

    pl.semaphore_wait(barrier, len(peers))
    signal(ring1, ring(1))
    signal(ring1, ring(-1))

    sends = []

    def copy(src, dst, send_sem, recv_sem, to):
        return pltpu.make_async_remote_copy(
            src_ref=src,
            dst_ref=dst,
            send_sem=send_sem,
            recv_sem=recv_sem,
            device_id=to,
            device_id_type=MESH,
        )

    def same(ref, send_sem, recv_sem, to):
        return copy(ref, ref, send_sem, recv_sem, to)

    def go(cp):
        cp.start()
        sends.append(cp)

    layers = [zl] + [(LAYER_CODE // 4 ** j // _power(zl)) % 4 for j in range(3)]

    def piece(k, layer, dp, dq, low, size):
        dx, dy = (dp, dq) if k == 0 else (dq, dp)
        return G.at[c, layer, xs[dx], ys[dy], pl.ds(k * 64 + low, size)]

    def first(j, k, d, dp):
        at = (j, k, DIR_AT[d])
        return same(piece(k, layers[j], dp, 0, 0, 64), s1_send.at[at], s1_recv.at[at], near[k, d])

    def first_far(j, k, dp):
        at = (j, k)
        return same(piece(k, layers[j], dp, 0, 0, 64), s2_send.at[at], s2_recv.at[at], far[k])

    def second(j, k, dp, d, dq):
        at = (j, k, PIECE_AT[dp], DIR_AT[d])
        return same(
            piece(k, layers[j], dp, dq, 0, 64), s3_send.at[at], s3_recv.at[at], near[1 - k, d]
        )

    def second_far(j, k, dp, d, dq):
        at = (j, k, PIECE_AT[dp], DIR_AT[d])
        low = 0 if d == 1 else 32
        return same(
            piece(k, layers[j], dp, dq, low, 32), s4_send.at[at], s4_recv.at[at], near[1 - k, d]
        )

    def step_begin(j):
        if j > 0:
            same(G.at[c, layers[j], x, y], z_send.at[0], z_recv.at[layers[j]], sibling).wait_recv()
        for d in DIRS:
            for k in CLASSES:
                go(first(j, k, d, 0))
        for k in CLASSES:
            go(first_far(j, k, 0))
        for d in DIRS:
            for k in CLASSES:
                go(second(j, k, 0, d, 0))

    def step_middle(j):
        for dp in (-1, 1):
            for d in DIRS:
                for k in CLASSES:
                    if d == 1:
                        first(j, k, -dp, dp).wait_recv()
                    go(second(j, k, dp, d, 0))
        for d in DIRS:
            for k in CLASSES:
                if d == 1:
                    first_far(j, k, 2).wait_recv()
                go(second(j, k, 2, d, 0))
        for k in CLASSES:
            go(to_sibling(c, j, k, 0))

    def step_end(j):
        for dp in (0, -1, 1, 2):
            for d in DIRS:
                for k in CLASSES:
                    second(j, k, dp, d, -d).wait_recv()
                    go(second_far(j, k, dp, d, -d))
        for d in DIRS:
            for k in CLASSES:
                go(to_sibling(c, j, k, d))

    def to_sibling(core, j, k, dq):
        if k == 0:
            ref = G.at[core, layers[j], :, ys[dq], pl.ds(0, 64)]
        else:
            ref = G.at[core, layers[j], xs[dq], :, pl.ds(64, 64)]
        at = (j, k, PIECE_AT[dq])
        return same(ref, sib_send.at[at], sib_recv.at[at], sibling)

    def step_finish(j):
        for k in CLASSES:
            for dp in (0, -1, 1, 2):
                for d in DIRS:
                    second_far(j, k, dp, d, 2).wait_recv()
            go(to_sibling(c, j, k, 2))

    mine = G.at[c, zl, x, y]
    for j, mate in enumerate(z_mates):
        go(same(mine, z_send.at[j], z_recv.at[zl], mate))

    step_begin(0)

    loads[2].wait()
    feat_t[rep] = (inv * feat_v[...].astype(F32)).T.astype(BF16)

    loads[3].wait()
    for load in loads[6:]:
        load.wait()
    count = count_ref[0, 0]

    def spread(s, carry):
        tile = tiles_v[s]
        live = s < count
        at = rows_ref[0, s]
        for r in range(4):
            stacked[r, :, pl.ds(pl.multiple_of(s * 128, 128), 128)] = jnp.where(
                jnp.logical_and(live, at == r), tile, jnp.zeros_like(tile)
            )
        return carry

    lax.fori_loop(0, SLOTS, spread, 0)

    def step_stage(n):
        if n == 0:
            pl.semaphore_wait(ring1, 2)
            signal(ring2, ring(2))
            signal(ring2, ring(-2))
        elif n == 1:
            pl.semaphore_wait(ring2, 2)
            signal(ring3, ring(4))
            signal(ring3, ring(-4))
        else:
            pl.semaphore_wait(ring3, 2)
            for j, mate in enumerate(rep_mates):
                go(same(feat_t.at[rep], feat_send.at[j], feat_recv.at[rep], mate))

    steps = {
        "begin": step_begin, "middle": step_middle, "end": step_end, "finish": step_finish,
        "stage": step_stage,
    }
    for name, j in STEPS[1:]:
        steps[name](j)
    for j in range(4):
        for k in CLASSES:
            for dq in (0, -1, 1, 2):
                to_sibling(1 - c, j, k, dq).wait_recv()

    for s in range(SLOTS):
        col = cols_ref[0, s]
        picked[pl.ds(s * 128, 128), :] = G[col % 2, col // 32, (col // 8) % 4, (col // 2) % 4]

    def multiply(r):
        return jnp.dot(stacked[r], picked[...], preferred_element_type=F32)

    def part_to(j):
        to = (rep + j) % 4
        return copy(part16.at[to], part_in.at[rep], part_send.at[j - 1], part_recv.at[rep], (row, to))

    gather_sends = list(sends)
    sends.clear()
    for j in (2, 1, 3):
        to = (rep + j) % 4
        part16[to] = multiply(to).astype(BF16)
        if j != 2:
            go(part_to(j))
    total[...] = multiply(rep)
    part16[rep] = total[...].astype(BF16)

    for j in (1, 2, 3):
        other = (rep + j) % 4
        same(feat_t.at[other], feat_send.at[0], feat_recv.at[other], sibling).wait_recv()
    term16 = jnp.dot(
        jnp.concatenate([feat_t[r] for r in range(4)], axis=1),
        jnp.concatenate([part16[r] for r in range(4)], axis=0),
        preferred_element_type=F32,
    ).astype(BF16)
    w16[0:16] = term16[:, 0:128].reshape(16, 16, 128)
    w16[16:32] = term16[:, 128:256].reshape(16, 16, 128)

    def wait_all(ref, count, sem):
        part = ref.at[pl.ds(0, count)]
        pltpu.make_async_copy(part, part, sem).wait()

    layer_mates = [xs[dx] * 8 + ys[dy] * 2 + (1 - c if dc else c) for dx, dy, dc in LAYER_OFFSETS]
    for to in layer_mates:
        copy(w16.at[to], w_in1.at[layer_at], w1_send, w1_recv, (zl * 32 + to, rep)).start()
    w_in1[layer_at] = w16[layer_at]
    wait_all(w_in1, 31, w1_recv)
    w_in2[z_at] = jnp.sum(w_in1[...].astype(F32), axis=0).astype(BF16)
    for j in RING_STEPS:
        copy(w_in2.at[z_at], w_in2.at[z_at], w2_send, w2_recv, ring(j)).start()
    go(part_to(2))
    wait_all(w16, 31, w1_send)
    for cp in gather_sends:
        cp.wait_send()
    wait_all(w_in2, 15, w2_recv)
    w_in3[layer_at] = jnp.sum(w_in2[...].astype(F32), axis=0).astype(BF16)
    for to in layer_mates:
        copy(w_in3.at[layer_at], w_in3.at[layer_at], w3_send, w3_recv, (zl * 32 + to, rep)).start()

    for j in (1, 2, 3):
        at = (rep + j) % 4
        copy(part16.at[0], part_in.at[at], part_send.at[0], part_recv.at[at], sibling).wait_recv()
    agg = total[...]
    for j in (1, 2, 3):
        agg += part_in[(rep + j) % 4].astype(F32)
    loads[4].wait()
    gf_out[...] = lax.dot_general(
        (inv * agg).astype(BF16), weight_v[...], (((1,), (1,)), ((), ())),
        preferred_element_type=F32,
    ).astype(BF16)
    for cp in sends:
        cp.wait_send()
    wait_all(w_in2, 15, w2_send)

    wait_all(w_in3, 31, w3_recv)
    gw_out[:, 0:128] = w_in3[0:16].astype(F32).reshape(256, 128)
    gw_out[:, 128:256] = w_in3[16:32].astype(F32).reshape(256, 128)
    wait_all(w_in3, 31, w3_send)


def _power(zl):
    return 1 + (zl >= 1) * 63 + (zl >= 2) * (64 * 63) + (zl >= 3) * (64 * 64 * 63)


def per_device(
    grad_out, pre_act, features, weight, tile_values, tile_rows, tile_cols, tile_count, degrees
):
    dma = pltpu.SemaphoreType.DMA
    regular = pltpu.SemaphoreType.REGULAR
    vmem = pltpu.VMEM
    any_spec = pl.BlockSpec(memory_space=pl.ANY)
    vmem_spec = pl.BlockSpec(memory_space=pltpu.VMEM)
    return pl.pallas_call(
        kernel,
        out_shape=(
            jax.ShapeDtypeStruct((128, 256), BF16),
            jax.ShapeDtypeStruct((256, 256), F32),
        ),
        in_specs=[any_spec] * 9,
        out_specs=(vmem_spec, vmem_spec),
        scratch_shapes=[
            pltpu.SMEM((1, SLOTS), jnp.int32),
            pltpu.SMEM((1, SLOTS), jnp.int32),
            pltpu.SMEM((1, 1), jnp.int32),
            vmem((1, 128), jnp.int32),
            vmem((2, 4, 4, 4, 128, 256), BF16),
            vmem((128, 256), BF16),
            vmem((128, 256), BF16),
            vmem((128, 256), BF16),
            vmem((256, 256), BF16),
            vmem((SLOTS, 128, 128), BF16),
            vmem((4, 128, SLOTS * 128), BF16),
            vmem((SLOTS * 128, 256), BF16),
            vmem((128, 256), F32),
            vmem((4, 256, 128), BF16),
            vmem((4, 128, 256), BF16),
            vmem((4, 128, 256), BF16),
            vmem((32, 16, 128), BF16),
            vmem((32, 16, 128), BF16),
            vmem((16, 16, 128), BF16),
            vmem((32, 16, 128), BF16),
            dma((9,)),
            dma((3,)), dma((4,)),
            dma((4, 2, 2)), dma((4, 2, 2)), dma((4, 2)), dma((4, 2)),
            dma((4, 2, 4, 2)), dma((4, 2, 4, 2)), dma((4, 2, 4, 2)), dma((4, 2, 4, 2)),
            dma((4, 2, 4)), dma((4, 2, 4)),
            dma((3,)), dma((4,)),
            dma((3,)), dma((4,)),
            dma, dma, dma, dma, dma, dma,
            regular, regular, regular,
        ],
        compiler_params=pltpu.CompilerParams(
            collective_id=0, has_side_effects=True, vmem_limit_bytes=62 * 2**20
        ),
    )(
        grad_out, pre_act, features, weight, tile_values[0, 0],
        tile_rows.reshape(1, SLOTS), tile_cols.reshape(1, SLOTS), tile_count,
        degrees.reshape(1, 128),
    )


def solution(mesh):
    in_specs = (
        P(("row", "rep"), None),
        P(("row", "rep"), None),
        P(("row", "rep"), None),
        P(),
        P("row", "rep", None, None, None),
        P("row", "rep", None),
        P("row", "rep", None),
        P("row", "rep"),
        P(("row", "rep")),
    )
    out_specs = (P(("row", "rep"), None), P())
    return jax.shard_map(
        per_device, mesh=mesh, in_specs=in_specs, out_specs=out_specs, check_vma=False
    )
```
